32 devices in a mesh: layer: 4 (over z), seq: 4 (over y, core), tile: 2 (over x).
Axes of the slice: x: 2, y: 2, z: 4, core: 2. Of those that a mesh axis runs over, the one named last changes fastest.
Arguments:
- activations: bfloat16 [16, 768, 4096], P('layer', 'seq', 'tile'), parts along dimension 0, may hold values from -6 to 6
- out_grads: bfloat16 [16, 768, 14336], P('layer', 'seq', 'tile'), parts along dimension 0, may hold values from -6 to 6
- proj_in: bfloat16 [16384, 128], P(('layer', 'tile')), parts along dimension 0, may hold values from -0.09375 to 0.09375
- proj_out: bfloat16 [57344, 256], P(('layer', 'tile')), parts along dimension 0, may hold values from -0.046875 to 0.046875
- seq_lengths: int32 [4], replicated, may hold values from 1 to 768, 1920 in all
- tile_map: int32 [8, 2], replicated, may hold values from 0 to 127, as said below
- prior_cov: float32 [32, 256, 256], P(('layer', 'seq', 'tile')), parts along dimension 0, may hold values from -6 to 6
Outputs:
- covariance: float32 [32, 256, 256], P(('layer', 'seq', 'tile')), parts along dimension 0
The draws below stay inside these ranges and needn't reach their ends.
There are 4 independent parts, one for each index of `layer`. The reference program is written for one: setup_inputs(seed, part) draws one part's arguments, and reference() takes and returns one part's arrays. A program takes and returns all parts, laid end to end along the dimension named above; an argument that names none is the same for every part. Nothing has to cross between parts.
Inputs may be any that keep to these rules, and one draw needn't show every extreme that they name: `tile_map`: each row holds two feature block numbers, the first not above the second; rows may repeat.
All inputs are finite; a program needn't handle non-finite values.
Results may differ from the reference program's by a relative error of at most 0.0003.
Values sent between devices are 32-bit elements; how exact they have to be, the bound alone decides.
A program may use at most 192 MiB of HBM per device.

```python
import math
import jax
import jax.numpy as jnp
import numpy as np
from jax import lax

D = 4096
FF = 14336
K_IN = 128
K_OUT = 256
TB = 256
SEQS = 4
LEN_DEV = 192
LEN = 768
NBLOCKS = 128
TILES = 8
N_SEQ = 4


def draw_tile_map(key, part):
    first_key, second_key = jax.random.split(jax.random.fold_in(key, 11))
    upper_draw = jax.random.randint(first_key, (TILES,), 0, NBLOCKS)
    lower_draw = jax.random.randint(second_key, (TILES,), 0, NBLOCKS)
    tile_rows = jnp.stack([jnp.minimum(upper_draw, lower_draw), jnp.maximum(upper_draw, lower_draw)], axis=1)
    tile_rows = tile_rows.at[0].set(jnp.array([0, NBLOCKS - 1], dtype=jnp.int32))
    return tile_rows.astype(jnp.int32)


def block_scale(own_key, extent, shards, low, largest):
    factor_of, own = 1.0, jax.random.fold_in(own_key, 6)
    for dim, shards_of in shards:
        heights = jnp.exp(jax.random.uniform(jax.random.fold_in(own, dim), (shards_of,), jnp.float32, low / len(shards), largest / len(shards)))
        factor_of = factor_of * jnp.repeat(heights, extent[dim] // shards_of).reshape([-1 if axis == dim else 1 for axis in range(len(extent))])
    return factor_of


def profile(count, total, most, lean):
    portions = [(1 << 20) // math.isqrt(rank ** lean) + 1 for rank in range(2, count + 1)]
    rest, holding = total - most - (count - 1), [1] * (count - 1)
    while rest > 0:
        movable = [i for i in range(count - 1) if holding[i] < most]
        mass, remaining = sum([portions[i] for i in movable]), rest
        for i in movable:
            addition = min(most - holding[i], max(1, remaining * portions[i] // mass), rest)
            holding[i] = holding[i] + addition
            rest = rest - addition
    return np.array([most] + holding)


def ragged(key, count, total, bound, slope):
    if count == 2:
        one = jax.random.randint(key, (), max(1, total - bound), min(bound, total - 1) + 1)
        return jnp.stack([one, total - one])
    sizes = jnp.asarray(profile(count, total, bound, slope), jnp.int32)
    twos = (count - 1) // 2
    source_of, sink = sizes[1:1 + 2 * twos:2], sizes[2:2 + 2 * twos:2]
    margin = jnp.minimum(source_of - 1, bound - sink)
    passed = jax.random.randint(jax.random.fold_in(key, 1), (twos,), 0, 1 << 20) % (margin + 1)
    sizes = sizes.at[1:1 + 2 * twos:2].set(source_of - passed).at[2:2 + 2 * twos:2].set(sink + passed)
    return sizes[jax.random.permutation(jax.random.fold_in(key, 2), count)]


def scatter_about(stream_key, extent, width, most, shards=(), kind=jnp.bfloat16):
    result = width * jax.random.normal(stream_key, extent, jnp.float32)
    if shards:
        result = result * block_scale(stream_key, extent, shards, -0.22, 0.18)
    return jnp.clip(result, -most, most).astype(kind)


def setup_inputs(seed: int = 0, part: int = 0) -> dict:
    splits = jax.random.split(jax.random.key(seed), 8)
    part_splits = jax.random.split(jax.random.fold_in(splits[7], part), 8)
    return {
        "activations": scatter_about(part_splits[0], (SEQS, LEN, D), 1.0, 6.0, ((1, 4), (2, 2))),
        "out_grads": scatter_about(part_splits[1], (SEQS, LEN, FF), 1.0, 6.0, ((1, 4), (2, 2))),
        "proj_in": scatter_about(part_splits[2], (D, K_IN), D ** -0.5, 0.09375, ((0, 2),)),
        "proj_out": scatter_about(part_splits[3], (FF, K_OUT), FF ** -0.5, 0.046875, ((0, 2),)),
        "seq_lengths": ragged(splits[4], SEQS, SEQS * LEN_DEV * N_SEQ * 5 // 8, LEN_DEV * N_SEQ, 1).astype(jnp.int32),
        "tile_map": draw_tile_map(jax.random.fold_in(splits[7], 71), part),
        "prior_cov": scatter_about(part_splits[6], (TILES, TB, TB), 1.0, 6.0, ((0, 8),), jnp.float32),
    }


def reference(activations, out_grads, proj_in, proj_out, seq_lengths, tile_map, prior_cov):
    positions = jnp.arange(LEN, dtype=jnp.int32)

    def one_sequence(inputs):
        seq_acts, seq_grads, length = inputs
        left_side = jnp.dot(seq_acts, proj_in, preferred_element_type=jnp.float32)
        right_side = jnp.dot(seq_grads, proj_out, preferred_element_type=jnp.float32)
        token_mask = (positions < length).astype(jnp.float32)
        right_side = right_side * token_mask[:, None]
        grad_matrix = jnp.dot(right_side.T, left_side, precision=lax.Precision.HIGHEST)
        grad_matrix = grad_matrix * lax.rsqrt(length.astype(jnp.float32))
        return grad_matrix.reshape(-1)
    example_grads = lax.map(one_sequence, (activations, out_grads, seq_lengths))
    blocks = example_grads.reshape(SEQS, NBLOCKS, TB)
    left_blocks = blocks[:, tile_map[:, 0], :]
    right_blocks = blocks[:, tile_map[:, 1], :]
    return prior_cov + jnp.einsum('ske,skf->kef', left_blocks, right_blocks, precision=lax.Precision.HIGHEST)
```

```python
import functools

import jax
import jax.numpy as jnp
from jax import lax
from jax.experimental import pallas as pl
from jax.experimental.pallas import tpu as pltpu
from jax.sharding import PartitionSpec as P

MESH = pl.DeviceIdType.MESH
F32 = jnp.float32
BF16 = jnp.bfloat16


def split_two(x):
    high = x.astype(BF16)
    return high, (x - high.astype(F32)).astype(BF16)


def dot_nt(a, b):
    return lax.dot_general(a, b, (((1,), (1,)), ((), ())), preferred_element_type=F32)


def kernel(
    seq_axis, tile_axis,
    lengths, tile_map, act_hbm, grad_hbm, pin_hbm, pout_hbm, prior_hbm,
    out_ref,
    act_v, grad_v, pin_v, pout_v, prior_v,
    picked, picked_in, acts, parts, parts_in, summed,
    load_sem, pick_send, pick_recv, part_send, part_recv,
):
    seqs, tok, _ = act_v.shape
    tiles = tile_map.shape[0]
    group = seq_axis * tile_axis
    here = tiles // group
    rows = 4 * tiles
    seq_me = lax.axis_index("seq")
    tile_me = lax.axis_index("tile")
    me = seq_me * tile_axis + tile_me

    loads = [pltpu.make_async_copy(pout_hbm, pout_v, load_sem.at[0])]
    for s in range(seqs):
        loads.append(pltpu.make_async_copy(grad_hbm.at[s], grad_v.at[s], load_sem.at[1 + s]))
    loads.append(pltpu.make_async_copy(pin_hbm, pin_v, load_sem.at[1 + seqs]))
    loads.append(pltpu.make_async_copy(act_hbm, act_v, load_sem.at[2 + seqs]))
    loads.append(pltpu.make_async_copy(prior_hbm, prior_v, load_sem.at[3 + seqs]))
    for load in loads:
        load.start()

    def peer(d):
        other = lax.rem(me + d, group)
        return other, {"seq": lax.div(other, tile_axis), "tile": lax.rem(other, tile_axis)}

    barrier = pltpu.get_barrier_semaphore()
    for d in range(1, group):
        pl.semaphore_signal(barrier, inc=1, device_id=peer(d)[1], device_id_type=MESH)

    width_out = pout_v.shape[1]
    width_in = pin_v.shape[1]
    per_block = out_ref.shape[1] // width_in
    row = lax.broadcasted_iota(jnp.int32, (rows, width_out), 0)
    column = lax.broadcasted_iota(jnp.int32, (rows, width_out), 1)
    wanted = jnp.zeros((rows, width_out), jnp.int32)
    for k in range(tiles):
        for side in range(2):
            wanted = jnp.where(row // per_block == 2 * k + side, tile_map[k, side], wanted)
    select = (column == wanted * per_block + row % per_block).astype(F32).astype(BF16)

    loads[0].wait()
    picks = []
    for s in range(seqs):
        loads[1 + s].wait()
        projected = jnp.dot(grad_v[s], pout_v[...], preferred_element_type=F32)
        high, low = split_two(projected)
        picked[s] = dot_nt(select, high) + dot_nt(select, low)
        if s == 0:
            pl.semaphore_wait(barrier, group - 1)
        for d in range(1, tile_axis):
            copy = pltpu.make_async_remote_copy(
                src_ref=picked.at[s],
                dst_ref=picked_in.at[d - 1, s],
                send_sem=pick_send.at[d - 1, s],
                recv_sem=pick_recv.at[d - 1, s],
                device_id={"tile": lax.rem(tile_me + d, tile_axis)},
                device_id_type=MESH,
            )
            copy.start()
            picks.append(copy)

    loads[1 + seqs].wait()
    loads[2 + seqs].wait()
    for s in range(seqs):
        acts[s] = jnp.dot(act_v[s], pin_v[...], preferred_element_type=F32)

    position = seq_me * tok + lax.broadcasted_iota(jnp.int32, (1, tok), 1)
    for s in range(seqs):
        total = picked[s]
        for d in range(1, tile_axis):
            picks[s * (tile_axis - 1) + d - 1].wait_recv()
            total = total + picked_in[d - 1, s]
        length = jnp.full((1, tok), lengths[s], jnp.int32)
        weight = jnp.where(position < length, lax.rsqrt(length.astype(F32)), 0.0)
        part = jnp.dot(
            total * weight, acts[s], precision=lax.Precision.HIGHEST, preferred_element_type=F32
        )
        for k in range(tiles):
            parts[k, 4 * s : 4 * s + 4, :] = part[4 * k : 4 * k + 4, :]

    moves = []
    for d in range(1, group):
        other, where = peer(d)
        copy = pltpu.make_async_remote_copy(
            src_ref=parts.at[pl.ds(other * here, here)],
            dst_ref=parts_in.at[d - 1],
            send_sem=part_send.at[d - 1],
            recv_sem=part_recv.at[d - 1],
            device_id=where,
            device_id_type=MESH,
        )
        copy.start()
        moves.append(copy)

    loads[3 + seqs].wait()
    total = parts[pl.ds(me * here, here)]
    for d in range(1, group):
        moves[d - 1].wait_recv()
        total = total + parts_in[d - 1]
    summed[...] = total
    for k in range(here):
        pieces = [summed[k, pl.ds(c, seqs, stride=4), :] for c in range(4)]
        left = jnp.concatenate(pieces[:2], axis=1)
        right = jnp.concatenate(pieces[2:], axis=1)
        product = lax.dot_general(
            left, right, (((0,), (0,)), ((), ())),
            precision=lax.Precision.HIGHEST, preferred_element_type=F32,
        )
        out_ref[k] = prior_v[k] + product
    for copy in picks:
        copy.wait_send()
    for copy in moves:
        copy.wait_send()


def body(seq_axis, tile_axis, activations, out_grads, proj_in, proj_out, seq_lengths, tile_map, prior_cov):
    seqs, tok, _ = activations.shape
    tiles = tile_map.shape[0]
    group = seq_axis * tile_axis
    here = prior_cov.shape[0]
    width_in = proj_in.shape[1]
    others = max(tile_axis - 1, 1)
    smem = pl.BlockSpec(memory_space=pltpu.SMEM)
    hbm = pl.BlockSpec(memory_space=pl.ANY)
    vmem = pl.BlockSpec(memory_space=pltpu.VMEM)
    return pl.pallas_call(
        functools.partial(kernel, seq_axis, tile_axis),
        out_shape=jax.ShapeDtypeStruct(prior_cov.shape, F32),
        in_specs=[smem, smem, hbm, hbm, hbm, hbm, hbm],
        out_specs=vmem,
        scratch_shapes=[
            pltpu.VMEM(activations.shape, BF16),
            pltpu.VMEM(out_grads.shape, BF16),
            pltpu.VMEM(proj_in.shape, BF16),
            pltpu.VMEM(proj_out.shape, BF16),
            pltpu.VMEM(prior_cov.shape, F32),
            pltpu.VMEM((seqs, 4 * tiles, tok), F32),
            pltpu.VMEM((others, seqs, 4 * tiles, tok), F32),
            pltpu.VMEM((seqs, tok, width_in), F32),
            pltpu.VMEM((tiles, 4 * seqs, width_in), F32),
            pltpu.VMEM((group - 1, here, 4 * seqs, width_in), F32),
            pltpu.VMEM((here, 4 * seqs, width_in), F32),
            pltpu.SemaphoreType.DMA((4 + seqs,)),
            pltpu.SemaphoreType.DMA((others, seqs)),
            pltpu.SemaphoreType.DMA((others, seqs)),
            pltpu.SemaphoreType.DMA((group - 1,)),
            pltpu.SemaphoreType.DMA((group - 1,)),
        ],
        compiler_params=pltpu.CompilerParams(
            collective_id=0, has_side_effects=True, vmem_limit_bytes=48 * 1024 * 1024
        ),
        name="grad_tiles",
    )(seq_lengths, tile_map, activations, out_grads, proj_in, proj_out, prior_cov)


def solution(mesh):
    return jax.shard_map(
        functools.partial(body, mesh.shape["seq"], mesh.shape["tile"]),
        mesh=mesh,
        in_specs=(
            P("layer", "seq", "tile"),
            P("layer", "seq", "tile"),
            P(("layer", "tile"), None),
            P(("layer", "tile"), None),
            P(),
            P(),
            P(("layer", "seq", "tile"), None, None),
        ),
        out_specs=P(("layer", "seq", "tile"), None, None),
        check_vma=False,
    )
```

```python
import functools

import jax
import jax.numpy as jnp
from jax import lax
from jax.experimental import pallas as pl
from jax.experimental.pallas import tpu as pltpu
from jax.sharding import PartitionSpec as P

MESH = pl.DeviceIdType.MESH
F32 = jnp.float32
BF16 = jnp.bfloat16


def split_two(x):
    high = x.astype(BF16)
    return high, (x - high.astype(F32)).astype(BF16)


def dot_nt(a, b):
    return lax.dot_general(a, b, (((1,), (1,)), ((), ())), preferred_element_type=F32)


def kernel(
    seq_axis, tile_axis,
    lengths, tile_map, act_hbm, grad_hbm, pin_hbm, pout_hbm, prior_hbm,
    out_ref,
    act_v, grad_v, pin_v, pout_v, prior_v,
    total_v, picked, picked_in, acts, parts, parts_in, summed,
    pout_sem, grad_sem, act_sem, rest_sem, pick_send, pick_recv, part_send, part_recv,
):
    seqs, tok, width = act_v.shape
    chunks, deep, width_out = pout_v.shape
    halves = act_sem.shape[0]
    per = seqs // halves
    tiles = tile_map.shape[1]
    group = seq_axis * tile_axis
    here = tiles // group
    rows = 4 * tiles
    seq_me = lax.axis_index("seq")
    tile_me = lax.axis_index("tile")
    me = seq_me * tile_axis + tile_me

    def load_pout(k):
        return pltpu.make_async_copy(
            pout_hbm.at[pl.ds(pl.multiple_of(k * deep, 128), deep)], pout_v.at[k], pout_sem.at[k]
        )

    def load_grad(h, k):
        return pltpu.make_async_copy(
            grad_hbm.at[pl.ds(h * per, per), :, pl.ds(pl.multiple_of(k * deep, 128), deep)],
            grad_v.at[k, pl.ds(h * per, per)],
            grad_sem.at[h, k],
        )

    def load_act(h):
        return pltpu.make_async_copy(
            act_hbm.at[pl.ds(h * per, per)], act_v.at[pl.ds(h * per, per)], act_sem.at[h]
        )

    load_pin = pltpu.make_async_copy(pin_hbm, pin_v, rest_sem.at[0])
    load_prior = pltpu.make_async_copy(prior_hbm, prior_v, rest_sem.at[1])
    for h in range(halves):
        for k in range(chunks):
            if h == 0:
                load_pout(k).start()
            load_grad(h, k).start()
    load_pin.start()
    for h in range(halves):
        load_act(h).start()
    load_prior.start()

    def peer(d):
        other = lax.rem(me + d, group)
        return other, {"seq": lax.div(other, tile_axis), "tile": lax.rem(other, tile_axis)}

    barrier = pltpu.get_barrier_semaphore()
    for d in range(1, group):
        pl.semaphore_signal(barrier, inc=1, device_id=peer(d)[1], device_id_type=MESH)

    width_in = pin_v.shape[1]
    per_block = out_ref.shape[1] // width_in
    row = lax.broadcasted_iota(jnp.int32, (rows, width_out), 0)
    column = lax.broadcasted_iota(jnp.int32, (rows, width_out), 1)
    wanted = jnp.zeros((rows, width_out), jnp.int32)
    for k in range(tiles):
        for side in range(2):
            wanted = jnp.where(row // per_block == 2 * k + side, tile_map[side, k], wanted)
    select = (column == wanted * per_block + row % per_block).astype(F32).astype(BF16)

    picks = []
    for h in range(halves):
        total_v[...] = jnp.zeros_like(total_v)

        @pl.loop(0, chunks)
        def _(k):
            if h == 0:
                load_pout(k).wait()
            load_grad(h, k).wait()
            block = grad_v[k, pl.ds(h * per, per)].reshape(per * tok, deep)
            total_v[...] += jnp.dot(block, pout_v[k], preferred_element_type=F32)

        for i in range(per):
            high, low = split_two(total_v[i * tok : (i + 1) * tok, :])
            picked[h * per + i] = dot_nt(select, high) + dot_nt(select, low)
        if h == 0:
            pl.semaphore_wait(barrier, group - 1)
        for d in range(1, tile_axis):
            copy = pltpu.make_async_remote_copy(
                src_ref=picked.at[pl.ds(h * per, per)],
                dst_ref=picked_in.at[d - 1, pl.ds(h * per, per)],
                send_sem=pick_send.at[d - 1, h],
                recv_sem=pick_recv.at[d - 1, h],
                device_id={"tile": lax.rem(tile_me + d, tile_axis)},
                device_id_type=MESH,
            )
            copy.start()
            picks.append(copy)

    load_pin.wait()
    for h in range(halves):
        load_act(h).wait()
        block = act_v[pl.ds(h * per, per)].reshape(per * tok, width)
        projected = jnp.dot(block, pin_v[...], preferred_element_type=F32)
        acts[pl.ds(h * per, per)] = jnp.concatenate(split_two(projected), axis=1).reshape(
            per, tok, 2 * width_in
        )

    position = seq_me * tok + lax.broadcasted_iota(jnp.int32, (1, tok), 1)
    for s in range(seqs):
        total = picked[s]
        for d in range(1, tile_axis):
            if s % per == 0:
                picks[s // per * (tile_axis - 1) + d - 1].wait_recv()
            total = total + picked_in[d - 1, s]
        length = jnp.full((1, tok), lengths[s], jnp.int32)
        weight = jnp.where(position < length, lax.rsqrt(length.astype(F32)), 0.0)
        high, low = split_two(total * weight)
        both = jnp.dot(high, acts[s], preferred_element_type=F32)
        part = both[:, :width_in] + both[:, width_in:]
        part = part + jnp.dot(low, acts[s, :, :width_in], preferred_element_type=F32)
        for k in range(tiles):
            parts[k, 4 * s : 4 * s + 4, :] = part[4 * k : 4 * k + 4, :]

    moves = []
    for d in range(1, group):
        other, where = peer(d)
        copy = pltpu.make_async_remote_copy(
            src_ref=parts.at[pl.ds(other * here, here)],
            dst_ref=parts_in.at[d - 1],
            send_sem=part_send.at[d - 1],
            recv_sem=part_recv.at[d - 1],
            device_id=where,
            device_id_type=MESH,
        )
        copy.start()
        moves.append(copy)

    load_prior.wait()
    total = parts[pl.ds(me * here, here)]
    for d in range(1, group):
        moves[d - 1].wait_recv()
        total = total + parts_in[d - 1]
    summed[...] = total
    for k in range(here):
        pieces = [summed[k, pl.ds(c, seqs, stride=4), :] for c in range(4)]
        left = jnp.concatenate(pieces[:2], axis=1)
        right = jnp.concatenate(pieces[2:], axis=1)
        product = lax.dot_general(
            left, right, (((0,), (0,)), ((), ())),
            precision=lax.Precision.HIGHEST, preferred_element_type=F32,
        )
        out_ref[k] = prior_v[k] + product
    for copy in picks:
        copy.wait_send()
    for copy in moves:
        copy.wait_send()


def body(seq_axis, tile_axis, activations, out_grads, proj_in, proj_out, seq_lengths, tile_map, prior_cov):
    seqs, tok, _ = activations.shape
    tiles = tile_map.shape[0]
    group = seq_axis * tile_axis
    here = prior_cov.shape[0]
    width_in = proj_in.shape[1]
    others = max(tile_axis - 1, 1)
    halves = 2 if seqs % 2 == 0 else 1
    depth = proj_out.shape[0]
    chunks = next(c for c in (4, 2, 1) if depth % (256 * c) == 0 or c == 1)
    deep = depth // chunks
    smem = pl.BlockSpec(memory_space=pltpu.SMEM)
    hbm = pl.BlockSpec(memory_space=pl.ANY)
    vmem = pl.BlockSpec(memory_space=pltpu.VMEM)
    return pl.pallas_call(
        functools.partial(kernel, seq_axis, tile_axis),
        out_shape=jax.ShapeDtypeStruct(prior_cov.shape, F32),
        in_specs=[smem, smem, hbm, hbm, hbm, hbm, hbm],
        out_specs=vmem,
        scratch_shapes=[
            pltpu.VMEM(activations.shape, BF16),
            pltpu.VMEM((chunks, seqs, tok, deep), BF16),
            pltpu.VMEM(proj_in.shape, BF16),
            pltpu.VMEM((chunks, deep, proj_out.shape[1]), BF16),
            pltpu.VMEM(prior_cov.shape, F32),
            pltpu.VMEM((seqs // halves * tok, proj_out.shape[1]), F32),
            pltpu.VMEM((seqs, 4 * tiles, tok), F32),
            pltpu.VMEM((others, seqs, 4 * tiles, tok), F32),
            pltpu.VMEM((seqs, tok, 2 * width_in), BF16),
            pltpu.VMEM((tiles, 4 * seqs, width_in), F32),
            pltpu.VMEM((group - 1, here, 4 * seqs, width_in), F32),
            pltpu.VMEM((here, 4 * seqs, width_in), F32),
            pltpu.SemaphoreType.DMA((chunks,)),
            pltpu.SemaphoreType.DMA((halves, chunks)),
            pltpu.SemaphoreType.DMA((halves,)),
            pltpu.SemaphoreType.DMA((2,)),
            pltpu.SemaphoreType.DMA((others, halves)),
            pltpu.SemaphoreType.DMA((others, halves)),
            pltpu.SemaphoreType.DMA((group - 1,)),
            pltpu.SemaphoreType.DMA((group - 1,)),
        ],
        compiler_params=pltpu.CompilerParams(
            collective_id=0, has_side_effects=True, vmem_limit_bytes=64 * 1024 * 1024
        ),
        name="grad_tiles",
    )(seq_lengths, tile_map.T, activations, out_grads, proj_in, proj_out, prior_cov)


def solution(mesh):
    return jax.shard_map(
        functools.partial(body, mesh.shape["seq"], mesh.shape["tile"]),
        mesh=mesh,
        in_specs=(
            P("layer", "seq", "tile"),
            P("layer", "seq", "tile"),
            P(("layer", "tile"), None),
            P(("layer", "tile"), None),
            P(),
            P(),
            P(("layer", "seq", "tile"), None, None),
        ),
        out_specs=P(("layer", "seq", "tile"), None, None),
        check_vma=False,
    )
```

```python
import functools

import jax
import jax.numpy as jnp
from jax import lax
from jax.experimental import pallas as pl
from jax.experimental.pallas import tpu as pltpu
from jax.sharding import PartitionSpec as P

MESH = pl.DeviceIdType.MESH
F32 = jnp.float32
BF16 = jnp.bfloat16


def split_two(x):
    high = x.astype(BF16)
    return high, (x - high.astype(F32)).astype(BF16)


def dot(a, b):
    return jnp.dot(a, b, preferred_element_type=F32)


def kernel(
    seq_axis, tile_axis,
    lengths_hbm, map_hbm, act_hbm, grad_hbm, pin_hbm, pout_hbm, prior_hbm,
    out_ref,
    lengths, tile_map, act_v, grad_v, pin_v, pout_v, prior_v,
    select_v, total_v, picked, picked_in, acts, parts, parts_in, stacked,
    pout_sem, grad_sem, act_sem, rest_sem, pick_send, pick_recv, part_send, part_recv,
):
    seqs, tok, width = act_v.shape
    chunks, deep, width_out = pout_v.shape
    halves = act_sem.shape[0]
    sub = tok // halves
    tiles = tile_map.shape[1]
    width_in = pin_v.shape[1]
    per_block = out_ref.shape[1] // width_in
    sides = 2 * per_block
    rows = sides * seqs
    lanes = tiles * rows
    group = seq_axis * tile_axis
    here = tiles // group
    seq_me = lax.axis_index("seq")
    tile_me = lax.axis_index("tile")
    me = seq_me * tile_axis + tile_me

    def load_pout(k):
        return pltpu.make_async_copy(
            pout_hbm.at[pl.ds(pl.multiple_of(k * deep, 128), deep)], pout_v.at[k], pout_sem.at[k]
        )

    def load_grad(h, k):
        return pltpu.make_async_copy(
            grad_hbm.at[:, pl.ds(h * sub, sub), pl.ds(pl.multiple_of(k * deep, 128), deep)],
            grad_v.at[k, :, pl.ds(h * sub, sub)],
            grad_sem.at[h, k],
        )

    def load_act(h):
        return pltpu.make_async_copy(
            act_hbm.at[:, pl.ds(h * sub, sub)], act_v.at[:, pl.ds(h * sub, sub)], act_sem.at[h]
        )

    load_map = pltpu.make_async_copy(map_hbm, tile_map, rest_sem.at[0])
    load_lengths = pltpu.make_async_copy(lengths_hbm, lengths, rest_sem.at[1])
    load_pin = pltpu.make_async_copy(pin_hbm, pin_v, rest_sem.at[2])
    load_prior = pltpu.make_async_copy(prior_hbm, prior_v, rest_sem.at[3])
    load_map.start()
    load_lengths.start()
    for h in range(halves):
        for k in range(chunks):
            if h == 0:
                load_pout(k).start()
            load_grad(h, k).start()
    load_pin.start()
    for h in range(halves):
        load_act(h).start()
    load_prior.start()

    def peer(d):
        other = lax.rem(me + d, group)
        return other, {"seq": lax.div(other, tile_axis), "tile": lax.rem(other, tile_axis)}

    barrier = pltpu.get_barrier_semaphore()
    for d in range(1, group):
        pl.semaphore_signal(barrier, inc=1, device_id=peer(d)[1], device_id_type=MESH)

    load_map.wait()
    load_lengths.wait()
    lane = lax.broadcasted_iota(jnp.int32, (1, lanes), 1)
    side = lane // seqs % sides
    wanted = jnp.zeros((1, lanes), jnp.int32)
    for k in range(tiles):
        block = jnp.where(side < per_block, tile_map[0, k], tile_map[1, k])
        wanted = jnp.where(lane // rows == k, block, wanted)
    wanted = wanted * per_block + side % per_block
    length = jnp.zeros((1, lanes), jnp.int32)
    for s in range(seqs):
        length = jnp.where(lane % seqs == s, lengths[s], length)
    scale = lax.rsqrt(length.astype(F32))
    column = lax.broadcasted_iota(jnp.int32, (width_out, lanes), 0)
    for s in range(seqs):
        match = jnp.where(column == wanted, 1.0, 0.0) * jnp.where(lane % seqs == s, 1.0, 0.0)
        select_v[s * width_out : (s + 1) * width_out, :] = match.astype(BF16)

    picks = []
    for h in range(halves):
        total_v[...] = jnp.zeros_like(total_v)

        @pl.loop(0, chunks)
        def _(k):
            if h == 0:
                load_pout(k).wait()
            load_grad(h, k).wait()
            block = grad_v[k, :, pl.ds(h * sub, sub)].reshape(seqs * sub, deep)
            total_v[...] += dot(block, pout_v[k])

        high, low = split_two(total_v[...])
        stack = jnp.concatenate(
            [
                jnp.concatenate([x[s * sub : (s + 1) * sub] for s in range(seqs)], axis=1)
                for x in (high, low)
            ],
            axis=0,
        )
        both = dot(stack, select_v[...])
        picked[h] = both[:sub] + both[sub:]
        if h == 0:
            pl.semaphore_wait(barrier, group - 1)
        for d in range(1, tile_axis):
            copy = pltpu.make_async_remote_copy(
                src_ref=picked.at[h],
                dst_ref=picked_in.at[d - 1, h],
                send_sem=pick_send.at[d - 1, h],
                recv_sem=pick_recv.at[d - 1, h],
                device_id={"tile": lax.rem(tile_me + d, tile_axis)},
                device_id_type=MESH,
            )
            copy.start()
            picks.append(copy)

    load_pin.wait()
    for h in range(halves):
        load_act(h).wait()
        block = act_v[:, pl.ds(h * sub, sub)].reshape(seqs * sub, width)
        split = split_two(dot(block, pin_v[...]))
        for j in range(2):
            for s in range(seqs):
                at = (j * seqs + s) * width_in
                acts[h, :, at : at + width_in] = split[j][s * sub : (s + 1) * sub]

    partial = jnp.zeros((lanes, seqs * width_in), F32)
    for h in range(halves):
        total = picked[h]
        for d in range(1, tile_axis):
            picks[h * (tile_axis - 1) + d - 1].wait_recv()
            total = total + picked_in[d - 1, h]
        position = seq_me * tok + h * sub + lax.broadcasted_iota(jnp.int32, (sub, lanes), 0)
        total = jnp.where(position < length, total * scale, 0.0)
        high, low = split_two(total.T)
        both = dot(high, acts[h])
        partial = partial + both[:, : seqs * width_in] + both[:, seqs * width_in :]
        partial = partial + dot(low, acts[h, :, : seqs * width_in])
    row = lax.broadcasted_iota(jnp.int32, (lanes, width_in), 0)
    own = jnp.zeros((lanes, width_in), F32)
    for s in range(seqs):
        own = jnp.where(row % seqs == s, partial[:, s * width_in : (s + 1) * width_in], own)
    parts[...] = own.reshape(tiles, rows, width_in)

    moves = []
    for d in range(1, group):
        other, where = peer(d)
        copy = pltpu.make_async_remote_copy(
            src_ref=parts.at[pl.ds(other * here, here)],
            dst_ref=parts_in.at[d - 1],
            send_sem=part_send.at[d - 1],
            recv_sem=part_recv.at[d - 1],
            device_id=where,
            device_id_type=MESH,
        )
        copy.start()
        moves.append(copy)

    load_prior.wait()
    total = parts[pl.ds(me * here, here)]
    for d in range(1, group):
        moves[d - 1].wait_recv()
        total = total + parts_in[d - 1]
    for k in range(here):
        pieces = [total[k, c * seqs : (c + 1) * seqs, :] for c in range(sides)]
        wide = [
            jnp.concatenate(pieces[:per_block], axis=1),
            jnp.concatenate(pieces[per_block:], axis=1),
        ]
        split = [[x.astype(F32) for x in split_two(side)] for side in wide]
        for j, part in enumerate((0, 1, 0)):
            stacked[0, j * seqs : (j + 1) * seqs, :] = split[0][part]
        for j, part in enumerate((0, 0, 1)):
            stacked[1, j * seqs : (j + 1) * seqs, :] = split[1][part]
        left = stacked[0].T.astype(BF16)
        out_ref[k] = prior_v[k] + dot(left, stacked[1].astype(BF16))
    for copy in picks:
        copy.wait_send()
    for copy in moves:
        copy.wait_send()


def body(seq_axis, tile_axis, activations, out_grads, proj_in, proj_out, seq_lengths, tile_map, prior_cov):
    seqs, tok, _ = activations.shape
    tiles = tile_map.shape[0]
    group = seq_axis * tile_axis
    here, block_size, _ = prior_cov.shape
    width_in = proj_in.shape[1]
    depth, width_out = proj_out.shape
    rows = 2 * (block_size // width_in) * seqs
    others = max(tile_axis - 1, 1)
    halves = 2 if tok % 32 == 0 else 1
    chunks = next(c for c in (4, 2, 1) if depth % (256 * c) == 0 or c == 1)
    sub, deep = tok // halves, depth // chunks
    hbm = pl.BlockSpec(memory_space=pltpu.HBM)
    vmem = pl.BlockSpec(memory_space=pltpu.VMEM)
    return pl.pallas_call(
        functools.partial(kernel, seq_axis, tile_axis),
        out_shape=jax.ShapeDtypeStruct(prior_cov.shape, F32),
        in_specs=[hbm] * 7,
        out_specs=vmem,
        scratch_shapes=[
            pltpu.SMEM(seq_lengths.shape, jnp.int32),
            pltpu.SMEM(tile_map.shape[::-1], jnp.int32),
            pltpu.VMEM(activations.shape, BF16),
            pltpu.VMEM((chunks, seqs, tok, deep), BF16),
            pltpu.VMEM(proj_in.shape, BF16),
            pltpu.VMEM((chunks, deep, width_out), BF16),
            pltpu.VMEM(prior_cov.shape, F32),
            pltpu.VMEM((seqs * width_out, tiles * rows), BF16),
            pltpu.VMEM((seqs * sub, width_out), F32),
            pltpu.VMEM((halves, sub, tiles * rows), F32),
            pltpu.VMEM((others, halves, sub, tiles * rows), F32),
            pltpu.VMEM((halves, sub, 2 * seqs * width_in), BF16),
            pltpu.VMEM((tiles, rows, width_in), F32),
            pltpu.VMEM((group - 1, here, rows, width_in), F32),
            pltpu.VMEM((2, 3 * seqs, block_size), F32),
            pltpu.SemaphoreType.DMA((chunks,)),
            pltpu.SemaphoreType.DMA((halves, chunks)),
            pltpu.SemaphoreType.DMA((halves,)),
            pltpu.SemaphoreType.DMA((4,)),
            pltpu.SemaphoreType.DMA((others, halves)),
            pltpu.SemaphoreType.DMA((others, halves)),
            pltpu.SemaphoreType.DMA((group - 1,)),
            pltpu.SemaphoreType.DMA((group - 1,)),
        ],
        compiler_params=pltpu.CompilerParams(
            collective_id=0, has_side_effects=True, vmem_limit_bytes=40 * 1024 * 1024
        ),
        name="grad_tiles",
    )(seq_lengths, tile_map.T, activations, out_grads, proj_in, proj_out, prior_cov)


def solution(mesh):
    return jax.shard_map(
        functools.partial(body, mesh.shape["seq"], mesh.shape["tile"]),
        mesh=mesh,
        in_specs=(
            P("layer", "seq", "tile"),
            P("layer", "seq", "tile"),
            P(("layer", "tile"), None),
            P(("layer", "tile"), None),
            P(),
            P(),
            P(("layer", "seq", "tile"), None, None),
        ),
        out_specs=P(("layer", "seq", "tile"), None, None),
        check_vma=False,
    )
```

```python
import functools

import jax
import jax.numpy as jnp
from jax import lax
from jax.experimental import pallas as pl
from jax.experimental.pallas import tpu as pltpu
from jax.sharding import PartitionSpec as P

MESH = pl.DeviceIdType.MESH
F32 = jnp.float32
BF16 = jnp.bfloat16


def split_two(x):
    high = x.astype(BF16)
    return high, (x - high.astype(F32)).astype(BF16)


def dot(a, b):
    return jnp.dot(a, b, preferred_element_type=F32)


def kernel(
    seq_axis, tile_axis,
    lengths_hbm, map_hbm, act_hbm, grad_hbm, pin_hbm, pout_hbm, prior_hbm,
    out_ref,
    lengths, tile_map, act_v, grad_v, pin_v, pout_v, prior_v,
    select_v, total_v, picked, picked_in, acts, parts, parts_in, stacked,
    pout_sem, grad_sem, act_sem, rest_sem, pick_send, pick_recv, part_send, part_recv,
):
    seqs, tok, width = act_v.shape
    chunks, deep, width_out = pout_v.shape
    halves = act_sem.shape[0]
    sub = tok // halves
    tiles = tile_map.shape[1]
    width_in = pin_v.shape[1]
    per_block = out_ref.shape[1] // width_in
    sides = 2 * per_block
    rows = sides * seqs
    lanes = tiles * rows
    group = seq_axis * tile_axis
    here = tiles // group
    seq_me = lax.axis_index("seq")
    tile_me = lax.axis_index("tile")
    me = seq_me * tile_axis + tile_me

    def load_pout(k):
        return pltpu.make_async_copy(
            pout_hbm.at[pl.ds(pl.multiple_of(k * deep, 128), deep)], pout_v.at[k], pout_sem.at[k]
        )

    def load_grad(h, k):
        return pltpu.make_async_copy(
            grad_hbm.at[:, pl.ds(h * sub, sub), pl.ds(pl.multiple_of(k * deep, 128), deep)],
            grad_v.at[k, :, pl.ds(h * sub, sub)],
            grad_sem.at[h, k],
        )

    def load_act(h):
        return pltpu.make_async_copy(
            act_hbm.at[:, pl.ds(h * sub, sub)], act_v.at[:, pl.ds(h * sub, sub)], act_sem.at[h]
        )

    load_map = pltpu.make_async_copy(map_hbm, tile_map, rest_sem.at[0])
    load_lengths = pltpu.make_async_copy(lengths_hbm, lengths, rest_sem.at[1])
    load_pin = pltpu.make_async_copy(pin_hbm, pin_v, rest_sem.at[2])
    load_prior = pltpu.make_async_copy(prior_hbm, prior_v, rest_sem.at[3])
    load_map.start()
    load_lengths.start()
    for h in range(halves):
        for k in range(chunks):
            if h == 0:
                load_pout(k).start()
            load_grad(h, k).start()
    load_pin.start()
    for h in range(halves):
        load_act(h).start()
    load_prior.start()

    def peer(d):
        other = lax.rem(me + d, group)
        return other, {"seq": lax.div(other, tile_axis), "tile": lax.rem(other, tile_axis)}

    barrier = pltpu.get_barrier_semaphore()
    for d in range(1, group):
        pl.semaphore_signal(barrier, inc=1, device_id=peer(d)[1], device_id_type=MESH)

    load_map.wait()
    load_lengths.wait()
    lane = lax.broadcasted_iota(jnp.int32, (1, lanes), 1)
    side = lane // seqs % sides
    wanted = jnp.zeros((1, lanes), jnp.int32)
    for k in range(tiles):
        block = jnp.where(side < per_block, tile_map[0, k], tile_map[1, k])
        wanted = jnp.where(lane // rows == k, block, wanted)
    wanted = wanted * per_block + side % per_block
    length = jnp.zeros((1, lanes), jnp.int32)
    for s in range(seqs):
        length = jnp.where(lane % seqs == s, lengths[s], length)
    scale = lax.rsqrt(length.astype(F32))
    column = lax.broadcasted_iota(jnp.int32, (width_out, lanes), 0)
    for s in range(seqs):
        match = jnp.where(column == wanted, 1.0, 0.0) * jnp.where(lane % seqs == s, 1.0, 0.0)
        select_v[s * width_out : (s + 1) * width_out, :] = match.astype(BF16)

    picks = []
    for h in range(halves):
        total_v[...] = jnp.zeros_like(total_v)

        @pl.loop(0, chunks)
        def _(k):
            if h == 0:
                load_pout(k).wait()
            load_grad(h, k).wait()
            block = grad_v[k, :, pl.ds(h * sub, sub)].reshape(seqs * sub, deep)
            total_v[...] += dot(block, pout_v[k])

        high, low = split_two(total_v[...])
        stack = jnp.concatenate(
            [
                jnp.concatenate([x[s * sub : (s + 1) * sub] for s in range(seqs)], axis=1)
                for x in (high, low)
            ],
            axis=0,
        )
        both = dot(stack, select_v[...])
        picked[h] = both[:sub] + both[sub:]
        if h == 0:
            pl.semaphore_wait(barrier, group - 1)
        for d in range(1, tile_axis):
            copy = pltpu.make_async_remote_copy(
                src_ref=picked.at[h],
                dst_ref=picked_in.at[d - 1, h],
                send_sem=pick_send.at[d - 1, h],
                recv_sem=pick_recv.at[d - 1, h],
                device_id={"tile": lax.rem(tile_me + d, tile_axis)},
                device_id_type=MESH,
            )
            copy.start()
            picks.append(copy)

    load_pin.wait()
    for h in range(halves):
        load_act(h).wait()
        block = act_v[:, pl.ds(h * sub, sub)].reshape(seqs * sub, width)
        split = split_two(dot(block, pin_v[...]))
        for j in range(2):
            for s in range(seqs):
                at = (j * seqs + s) * width_in
                acts[h, :, at : at + width_in] = split[j][s * sub : (s + 1) * sub]

    partial = jnp.zeros((lanes, seqs * width_in), F32)
    for h in range(halves):
        total = picked[h]
        for d in range(1, tile_axis):
            picks[h * (tile_axis - 1) + d - 1].wait_recv()
            total = total + picked_in[d - 1, h]
        position = seq_me * tok + h * sub + lax.broadcasted_iota(jnp.int32, (sub, lanes), 0)
        total = jnp.where(position < length, total * scale, 0.0)
        high, low = split_two(total.T)
        both = dot(high, acts[h])
        partial = partial + both[:, : seqs * width_in] + both[:, seqs * width_in :]
        partial = partial + dot(low, acts[h, :, : seqs * width_in])
    row = lax.broadcasted_iota(jnp.int32, (lanes, width_in), 0)
    own = jnp.zeros((lanes, width_in), F32)
    for s in range(seqs):
        own = jnp.where(row % seqs == s, partial[:, s * width_in : (s + 1) * width_in], own)
    parts[...] = own.reshape(tiles, rows, width_in)

    moves = []
    for d in range(1, group):
        other, where = peer(d)
        copy = pltpu.make_async_remote_copy(
            src_ref=parts.at[pl.ds(other * here, here)],
            dst_ref=parts_in.at[d - 1],
            send_sem=part_send.at[d - 1],
            recv_sem=part_recv.at[d - 1],
            device_id=where,
            device_id_type=MESH,
        )
        copy.start()
        moves.append(copy)

    load_prior.wait()
    total = parts[pl.ds(me * here, here)]
    for d in range(1, group):
        moves[d - 1].wait_recv()
        total = total + parts_in[d - 1]
    for k in range(here):
        pieces = [total[k, c * seqs : (c + 1) * seqs, :] for c in range(sides)]
        wide = [
            jnp.concatenate(pieces[:per_block], axis=1),
            jnp.concatenate(pieces[per_block:], axis=1),
        ]
        split = [[x.astype(F32) for x in split_two(side)] for side in wide]
        for j, part in enumerate((0, 1, 0)):
            stacked[0, j * seqs : (j + 1) * seqs, :] = split[0][part]
        for j, part in enumerate((0, 0, 1)):
            stacked[1, j * seqs : (j + 1) * seqs, :] = split[1][part]
        left = stacked[0].T.astype(BF16)
        out_ref[k] = prior_v[k] + dot(left, stacked[1].astype(BF16))
    for copy in picks:
        copy.wait_send()
    for copy in moves:
        copy.wait_send()


def body(seq_axis, tile_axis, activations, out_grads, proj_in, proj_out, seq_lengths, tile_map, prior_cov):
    seqs, tok, _ = activations.shape
    tiles = tile_map.shape[0]
    group = seq_axis * tile_axis
    here, block_size, _ = prior_cov.shape
    width_in = proj_in.shape[1]
    depth, width_out = proj_out.shape
    rows = 2 * (block_size // width_in) * seqs
    others = max(tile_axis - 1, 1)
    halves = 2 if tok % 32 == 0 else 1
    chunks = next(c for c in (4, 2, 1) if depth % (256 * c) == 0 or c == 1)
    sub, deep = tok // halves, depth // chunks
    hbm = pl.BlockSpec(memory_space=pltpu.HBM)
    vmem = pl.BlockSpec(memory_space=pltpu.VMEM)
    return pl.pallas_call(
        functools.partial(kernel, seq_axis, tile_axis),
        out_shape=pltpu.VMEM(prior_cov.shape, F32),
        in_specs=[hbm] * 7,
        out_specs=vmem,
        scratch_shapes=[
            pltpu.SMEM(seq_lengths.shape, jnp.int32),
            pltpu.SMEM(tile_map.shape[::-1], jnp.int32),
            pltpu.VMEM(activations.shape, BF16),
            pltpu.VMEM((chunks, seqs, tok, deep), BF16),
            pltpu.VMEM(proj_in.shape, BF16),
            pltpu.VMEM((chunks, deep, width_out), BF16),
            pltpu.VMEM(prior_cov.shape, F32),
            pltpu.VMEM((seqs * width_out, tiles * rows), BF16),
            pltpu.VMEM((seqs * sub, width_out), F32),
            pltpu.VMEM((halves, sub, tiles * rows), F32),
            pltpu.VMEM((others, halves, sub, tiles * rows), F32),
            pltpu.VMEM((halves, sub, 2 * seqs * width_in), BF16),
            pltpu.VMEM((tiles, rows, width_in), F32),
            pltpu.VMEM((group - 1, here, rows, width_in), F32),
            pltpu.VMEM((2, 3 * seqs, block_size), F32),
            pltpu.SemaphoreType.DMA((chunks,)),
            pltpu.SemaphoreType.DMA((halves, chunks)),
            pltpu.SemaphoreType.DMA((halves,)),
            pltpu.SemaphoreType.DMA((4,)),
            pltpu.SemaphoreType.DMA((others, halves)),
            pltpu.SemaphoreType.DMA((others, halves)),
            pltpu.SemaphoreType.DMA((group - 1,)),
            pltpu.SemaphoreType.DMA((group - 1,)),
        ],
        compiler_params=pltpu.CompilerParams(
            collective_id=0, has_side_effects=True, vmem_limit_bytes=48 * 1024 * 1024
        ),
        name="grad_tiles",
    )(
        *(
            pltpu.with_memory_space_constraint(x, pltpu.HBM)
            for x in (seq_lengths, tile_map.T, activations, out_grads, proj_in, proj_out, prior_cov)
        )
    )


def solution(mesh):
    return jax.shard_map(
        functools.partial(body, mesh.shape["seq"], mesh.shape["tile"]),
        mesh=mesh,
        in_specs=(
            P("layer", "seq", "tile"),
            P("layer", "seq", "tile"),
            P(("layer", "tile"), None),
            P(("layer", "tile"), None),
            P(),
            P(),
            P(("layer", "seq", "tile"), None, None),
        ),
        out_specs=P(("layer", "seq", "tile"), None, None),
        check_vma=False,
    )
```

```python
import functools

import jax
import jax.numpy as jnp
from jax import lax
from jax.experimental import pallas as pl
from jax.experimental.pallas import tpu as pltpu
from jax.sharding import PartitionSpec as P

MESH = pl.DeviceIdType.MESH
F32 = jnp.float32
BF16 = jnp.bfloat16
AHEAD = 3


def split_two(x):
    high = x.astype(BF16)
    return high, (x - high.astype(F32)).astype(BF16)


def dot(a, b):
    return jnp.dot(a, b, preferred_element_type=F32)


def kernel(
    seq_axis, tile_axis,
    lengths_hbm, map_hbm, act_hbm, grad_hbm, pin_hbm, pout_hbm, prior_hbm,
    out_ref,
    lengths, tile_map, act_v, grad_v, pin_v, pout_v, prior_v,
    select_v, total_v, picked, picked_in, acts, parts, parts_in, stacked,
    pout_sem, grad_sem, act_sem, rest_sem, pick_send, pick_recv, part_send, part_recv,
):
    seqs, tok, width = act_v.shape
    chunks, deep, width_out = pout_v.shape
    halves = act_sem.shape[0]
    sub = tok // halves
    tiles = tile_map.shape[1]
    width_in = pin_v.shape[1]
    per_block = out_ref.shape[1] // width_in
    sides = 2 * per_block
    rows = sides * seqs
    lanes = tiles * rows
    group = seq_axis * tile_axis
    here = tiles // group
    seq_me = lax.axis_index("seq")
    tile_me = lax.axis_index("tile")
    me = seq_me * tile_axis + tile_me

    def load_pout(k):
        return pltpu.make_async_copy(
            pout_hbm.at[pl.ds(pl.multiple_of(k * deep, 128), deep)], pout_v.at[k], pout_sem.at[k]
        )

    def load_grad(k):
        return pltpu.make_async_copy(
            grad_hbm.at[:, :, pl.ds(pl.multiple_of(k * deep, 128), deep)], grad_v.at[k], grad_sem.at[k]
        )

    def load_act(h):
        return pltpu.make_async_copy(
            act_hbm.at[:, pl.ds(h * sub, sub)], act_v.at[:, pl.ds(h * sub, sub)], act_sem.at[h]
        )

    load_map = pltpu.make_async_copy(map_hbm, tile_map, rest_sem.at[0])
    load_lengths = pltpu.make_async_copy(lengths_hbm, lengths, rest_sem.at[1])
    load_pin = pltpu.make_async_copy(pin_hbm, pin_v, rest_sem.at[2])
    load_prior = pltpu.make_async_copy(prior_hbm, prior_v, rest_sem.at[3])
    load_map.start()
    load_lengths.start()
    for k in range(min(AHEAD, chunks)):
        load_pout(k).start()
        load_grad(k).start()

    def peer(d):
        other = lax.rem(me + d, group)
        return other, {"seq": lax.div(other, tile_axis), "tile": lax.rem(other, tile_axis)}

    barrier = pltpu.get_barrier_semaphore()
    for d in range(1, group):
        pl.semaphore_signal(barrier, inc=1, device_id=peer(d)[1], device_id_type=MESH)

    load_map.wait()
    load_lengths.wait()
    lane = lax.broadcasted_iota(jnp.int32, (1, lanes), 1)
    side = lane // seqs % sides
    wanted = jnp.zeros((1, lanes), jnp.int32)
    for k in range(tiles):
        block = jnp.where(side < per_block, tile_map[0, k], tile_map[1, k])
        wanted = jnp.where(lane // rows == k, block, wanted)
    wanted = wanted * per_block + side % per_block
    length = jnp.zeros((1, lanes), jnp.int32)
    for s in range(seqs):
        length = jnp.where(lane % seqs == s, lengths[s], length)
    scale = lax.rsqrt(length.astype(F32))
    column = lax.broadcasted_iota(jnp.int32, (width_out, lanes), 0)
    for s in range(seqs):
        match = jnp.where(column == wanted, 1.0, 0.0) * jnp.where(lane % seqs == s, 1.0, 0.0)
        select_v[s * width_out : (s + 1) * width_out, :] = match.astype(BF16)

    total_v[...] = jnp.zeros_like(total_v)

    @pl.loop(0, chunks)
    def _(k):
        load_pout(k).wait()
        load_grad(k).wait()

        @pl.when(k + AHEAD < chunks)
        def _():
            load_pout(k + AHEAD).start()
            load_grad(k + AHEAD).start()

        @pl.when(k == max(chunks - AHEAD, 0))
        def _():
            load_pin.start()
            for h in range(halves):
                load_act(h).start()
            load_prior.start()

        total_v[...] += dot(grad_v[k].reshape(seqs * tok, deep), pout_v[k])

    picks = []
    for h in range(halves):
        begin = [s * tok + h * sub for s in range(seqs)]
        wide = jnp.concatenate([total_v[at : at + sub, :] for at in begin], axis=1)
        stack = jnp.concatenate(split_two(wide), axis=0)
        both = dot(stack, select_v[...])
        picked[h] = both[:sub] + both[sub:]
        if h == 0:
            pl.semaphore_wait(barrier, group - 1)
        for d in range(1, tile_axis):
            copy = pltpu.make_async_remote_copy(
                src_ref=picked.at[h],
                dst_ref=picked_in.at[d - 1, h],
                send_sem=pick_send.at[d - 1, h],
                recv_sem=pick_recv.at[d - 1, h],
                device_id={"tile": lax.rem(tile_me + d, tile_axis)},
                device_id_type=MESH,
            )
            copy.start()
            picks.append(copy)

    load_pin.wait()
    for h in range(halves):
        load_act(h).wait()
        block = act_v[:, pl.ds(h * sub, sub)].reshape(seqs * sub, width)
        split = split_two(dot(block, pin_v[...]))
        for j in range(2):
            for s in range(seqs):
                at = (j * seqs + s) * width_in
                acts[h, :, at : at + width_in] = split[j][s * sub : (s + 1) * sub]

    partial = jnp.zeros((lanes, seqs * width_in), F32)
    for h in range(halves):
        total = picked[h]
        for d in range(1, tile_axis):
            picks[h * (tile_axis - 1) + d - 1].wait_recv()
            total = total + picked_in[d - 1, h]
        position = seq_me * tok + h * sub + lax.broadcasted_iota(jnp.int32, (sub, lanes), 0)
        total = jnp.where(position < length, total * scale, 0.0)
        high, low = split_two(total.T)
        both = dot(high, acts[h])
        partial = partial + both[:, : seqs * width_in] + both[:, seqs * width_in :]
        partial = partial + dot(low, acts[h, :, : seqs * width_in])
    row = lax.broadcasted_iota(jnp.int32, (lanes, width_in), 0)
    own = jnp.zeros((lanes, width_in), F32)
    for s in range(seqs):
        own = jnp.where(row % seqs == s, partial[:, s * width_in : (s + 1) * width_in], own)
    parts[...] = own.reshape(tiles, rows, width_in)

    moves = []
    for d in range(1, group):
        other, where = peer(d)
        copy = pltpu.make_async_remote_copy(
            src_ref=parts.at[pl.ds(other * here, here)],
            dst_ref=parts_in.at[d - 1],
            send_sem=part_send.at[d - 1],
            recv_sem=part_recv.at[d - 1],
            device_id=where,
            device_id_type=MESH,
        )
        copy.start()
        moves.append(copy)

    load_prior.wait()
    total = parts[pl.ds(me * here, here)]
    for d in range(1, group):
        moves[d - 1].wait_recv()
        total = total + parts_in[d - 1]
    for k in range(here):
        pieces = [total[k, c * seqs : (c + 1) * seqs, :] for c in range(sides)]
        wide = [
            jnp.concatenate(pieces[:per_block], axis=1),
            jnp.concatenate(pieces[per_block:], axis=1),
        ]
        split = [[x.astype(F32) for x in split_two(side)] for side in wide]
        for j, part in enumerate((0, 1, 0)):
            stacked[0, j * seqs : (j + 1) * seqs, :] = split[0][part]
        for j, part in enumerate((0, 0, 1)):
            stacked[1, j * seqs : (j + 1) * seqs, :] = split[1][part]
        left = stacked[0].T.astype(BF16)
        out_ref[k] = prior_v[k] + dot(left, stacked[1].astype(BF16))
    for copy in picks:
        copy.wait_send()
    for copy in moves:
        copy.wait_send()


def body(seq_axis, tile_axis, activations, out_grads, proj_in, proj_out, seq_lengths, tile_map, prior_cov):
    seqs, tok, _ = activations.shape
    tiles = tile_map.shape[0]
    group = seq_axis * tile_axis
    here, block_size, _ = prior_cov.shape
    width_in = proj_in.shape[1]
    depth, width_out = proj_out.shape
    rows = 2 * (block_size // width_in) * seqs
    others = max(tile_axis - 1, 1)
    halves = 2 if tok % 32 == 0 else 1
    chunks = next(c for c in (7, 4, 2, 1) if depth % (256 * c) == 0 or c == 1)
    sub, deep = tok // halves, depth // chunks
    hbm = pl.BlockSpec(memory_space=pltpu.HBM)
    vmem = pl.BlockSpec(memory_space=pltpu.VMEM)
    return pl.pallas_call(
        functools.partial(kernel, seq_axis, tile_axis),
        out_shape=pltpu.VMEM(prior_cov.shape, F32),
        in_specs=[hbm] * 7,
        out_specs=vmem,
        scratch_shapes=[
            pltpu.SMEM(seq_lengths.shape, jnp.int32),
            pltpu.SMEM(tile_map.shape[::-1], jnp.int32),
            pltpu.VMEM(activations.shape, BF16),
            pltpu.VMEM((chunks, seqs, tok, deep), BF16),
            pltpu.VMEM(proj_in.shape, BF16),
            pltpu.VMEM((chunks, deep, width_out), BF16),
            pltpu.VMEM(prior_cov.shape, F32),
            pltpu.VMEM((seqs * width_out, tiles * rows), BF16),
            pltpu.VMEM((seqs * tok, width_out), F32),
            pltpu.VMEM((halves, sub, tiles * rows), F32),
            pltpu.VMEM((others, halves, sub, tiles * rows), F32),
            pltpu.VMEM((halves, sub, 2 * seqs * width_in), BF16),
            pltpu.VMEM((tiles, rows, width_in), F32),
            pltpu.VMEM((group - 1, here, rows, width_in), F32),
            pltpu.VMEM((2, 3 * seqs, block_size), F32),
            pltpu.SemaphoreType.DMA((chunks,)),
            pltpu.SemaphoreType.DMA((chunks,)),
            pltpu.SemaphoreType.DMA((halves,)),
            pltpu.SemaphoreType.DMA((4,)),
            pltpu.SemaphoreType.DMA((others, halves)),
            pltpu.SemaphoreType.DMA((others, halves)),
            pltpu.SemaphoreType.DMA((group - 1,)),
            pltpu.SemaphoreType.DMA((group - 1,)),
        ],
        compiler_params=pltpu.CompilerParams(
            collective_id=0, has_side_effects=True, vmem_limit_bytes=48 * 1024 * 1024
        ),
        name="grad_tiles",
    )(
        *(
            pltpu.with_memory_space_constraint(x, pltpu.HBM)
            for x in (seq_lengths, tile_map.T, activations, out_grads, proj_in, proj_out, prior_cov)
        )
    )


def solution(mesh):
    return jax.shard_map(
        functools.partial(body, mesh.shape["seq"], mesh.shape["tile"]),
        mesh=mesh,
        in_specs=(
            P("layer", "seq", "tile"),
            P("layer", "seq", "tile"),
            P(("layer", "tile"), None),
            P(("layer", "tile"), None),
            P(),
            P(),
            P(("layer", "seq", "tile"), None, None),
        ),
        out_specs=P(("layer", "seq", "tile"), None, None),
        check_vma=False,
    )
```

```python
import functools

import jax
import jax.numpy as jnp
from jax import lax
from jax.experimental import pallas as pl
from jax.experimental.pallas import tpu as pltpu
from jax.sharding import PartitionSpec as P

MESH = pl.DeviceIdType.MESH
F32 = jnp.float32
BF16 = jnp.bfloat16


def split_two(x):
    high = x.astype(BF16)
    return high, (x - high.astype(F32)).astype(BF16)


def dot(a, b):
    return jnp.dot(a, b, preferred_element_type=F32)


def kernel(
    seq_axis, tile_axis,
    lengths_hbm, map_hbm, act_hbm, grad_hbm, pin_hbm, pout_hbm, prior_hbm,
    out_ref,
    lengths, tile_map, act_v, grad_v, pin_v, pout_v, prior_v,
    select_v, chosen_v, total_v, spread, picked, picked_in, acts, parts, parts_in, stacked,
    pout_sem, grad_sem, act_sem, rest_sem, pick_send, pick_recv, part_send, part_recv,
):
    seqs, tok, width = act_v.shape
    chunks, deep, width_out = pout_v.shape
    halves = act_sem.shape[0]
    sub = tok // halves
    tiles = tile_map.shape[1]
    width_in = pin_v.shape[1]
    per_block = out_ref.shape[1] // width_in
    sides = 2 * per_block
    rows = sides * seqs
    lanes = tiles * rows
    group = seq_axis * tile_axis
    here = tiles // group
    seq_me = lax.axis_index("seq")
    tile_me = lax.axis_index("tile")
    me = seq_me * tile_axis + tile_me

    def load_pout(k):
        return pltpu.make_async_copy(
            pout_hbm.at[pl.ds(pl.multiple_of(k * deep, 128), deep)], pout_v.at[k], pout_sem.at[k]
        )

    def load_grad(h, k):
        return pltpu.make_async_copy(
            grad_hbm.at[:, pl.ds(h * sub, sub), pl.ds(pl.multiple_of(k * deep, 128), deep)],
            grad_v.at[k, :, pl.ds(h * sub, sub)],
            grad_sem.at[h, k],
        )

    def load_act(h):
        return pltpu.make_async_copy(
            act_hbm.at[:, pl.ds(h * sub, sub)], act_v.at[:, pl.ds(h * sub, sub)], act_sem.at[h]
        )

    load_map = pltpu.make_async_copy(map_hbm, tile_map, rest_sem.at[0])
    load_lengths = pltpu.make_async_copy(lengths_hbm, lengths, rest_sem.at[1])
    load_pin = pltpu.make_async_copy(pin_hbm, pin_v, rest_sem.at[2])
    load_prior = pltpu.make_async_copy(prior_hbm, prior_v, rest_sem.at[3])
    load_map.start()
    load_lengths.start()
    for h in range(halves):
        for k in range(chunks):
            if h == 0:
                load_pout(k).start()
            load_grad(h, k).start()
    load_pin.start()
    for h in range(halves):
        load_act(h).start()
    load_prior.start()

    def peer(d):
        other = lax.rem(me + d, group)
        return other, {"seq": lax.div(other, tile_axis), "tile": lax.rem(other, tile_axis)}

    barrier = pltpu.get_barrier_semaphore()
    for d in range(1, group):
        pl.semaphore_signal(barrier, inc=1, device_id=peer(d)[1], device_id_type=MESH)

    load_map.wait()
    load_lengths.wait()
    lane = lax.broadcasted_iota(jnp.int32, (1, lanes), 1)
    side = lane // seqs % sides
    wanted = jnp.zeros((1, lanes), jnp.int32)
    for k in range(tiles):
        block = jnp.where(side < per_block, tile_map[0, k], tile_map[1, k])
        wanted = jnp.where(lane // rows == k, block, wanted)
    wanted = wanted * per_block + side % per_block
    length = jnp.zeros((1, lanes), jnp.int32)
    for s in range(seqs):
        length = jnp.where(lane % seqs == s, lengths[s], length)
    scale = lax.rsqrt(length.astype(F32))
    column = lax.broadcasted_iota(jnp.int32, (width_out, lanes), 0)
    select_v[...] = jnp.where(column == wanted, 1.0, 0.0).astype(BF16)

    picks = []
    for h in range(halves):
        total_v[...] = jnp.zeros_like(total_v)

        @pl.loop(0, chunks)
        def _(k):
            if h == 0:
                load_pout(k).wait()
                chosen_v[k] = dot(pout_v[k], select_v[...]).astype(BF16)
            load_grad(h, k).wait()
            block = grad_v[k, :, pl.ds(h * sub, sub)].reshape(seqs * sub, deep)
            total_v[...] += dot(block, chosen_v[k])

        mine = jnp.zeros((sub, lanes), F32)
        for s in range(seqs):
            mine = jnp.where(lane % seqs == s, total_v[s * sub : (s + 1) * sub, :], mine)
        picked[h] = mine
        if h == 0:
            pl.semaphore_wait(barrier, group - 1)
        for d in range(1, tile_axis):
            copy = pltpu.make_async_remote_copy(
                src_ref=picked.at[h],
                dst_ref=picked_in.at[d - 1, h],
                send_sem=pick_send.at[d - 1, h],
                recv_sem=pick_recv.at[d - 1, h],
                device_id={"tile": lax.rem(tile_me + d, tile_axis)},
                device_id_type=MESH,
            )
            copy.start()
            picks.append(copy)

    load_pin.wait()
    for h in range(halves):
        load_act(h).wait()
        block = act_v[:, pl.ds(h * sub, sub)].reshape(seqs * sub, width)
        acts[h] = jnp.concatenate(split_two(dot(block, pin_v[...])), axis=1)

    own = jnp.zeros((lanes, width_in), F32)
    row = lax.broadcasted_iota(jnp.int32, (lanes, sub), 0)
    for h in range(halves):
        total = picked[h]
        for d in range(1, tile_axis):
            picks[h * (tile_axis - 1) + d - 1].wait_recv()
            total = total + picked_in[d - 1, h]
        position = seq_me * tok + h * sub + lax.broadcasted_iota(jnp.int32, (sub, lanes), 0)
        total = jnp.where(position < length, total * scale, 0.0)
        turned = total.T
        split = [split_two(jnp.where(row % seqs == s, turned, 0.0)) for s in range(seqs)]
        for j in range(2):
            for s in range(seqs):
                spread[j * lanes : (j + 1) * lanes, s * sub : (s + 1) * sub] = split[s][j]
        both = dot(spread[...], acts[h])
        own = own + both[:lanes, :width_in]
        own = own + both[:lanes, width_in:] + both[lanes:, :width_in]
    parts[...] = own.reshape(tiles, rows, width_in)

    moves = []
    for d in range(1, group):
        other, where = peer(d)
        copy = pltpu.make_async_remote_copy(
            src_ref=parts.at[pl.ds(other * here, here)],
            dst_ref=parts_in.at[d - 1],
            send_sem=part_send.at[d - 1],
            recv_sem=part_recv.at[d - 1],
            device_id=where,
            device_id_type=MESH,
        )
        copy.start()
        moves.append(copy)

    load_prior.wait()
    total = parts[pl.ds(me * here, here)]
    for d in range(1, group):
        moves[d - 1].wait_recv()
        total = total + parts_in[d - 1]
    for k in range(here):
        pieces = [total[k, c * seqs : (c + 1) * seqs, :] for c in range(sides)]
        wide = [
            jnp.concatenate(pieces[:per_block], axis=1),
            jnp.concatenate(pieces[per_block:], axis=1),
        ]
        split = [[x.astype(F32) for x in split_two(side)] for side in wide]
        for j, part in enumerate((0, 1, 0)):
            stacked[0, j * seqs : (j + 1) * seqs, :] = split[0][part]
        for j, part in enumerate((0, 0, 1)):
            stacked[1, j * seqs : (j + 1) * seqs, :] = split[1][part]
        left = stacked[0].T.astype(BF16)
        out_ref[k] = prior_v[k] + dot(left, stacked[1].astype(BF16))
    for copy in picks:
        copy.wait_send()
    for copy in moves:
        copy.wait_send()


def body(seq_axis, tile_axis, activations, out_grads, proj_in, proj_out, seq_lengths, tile_map, prior_cov):
    seqs, tok, _ = activations.shape
    tiles = tile_map.shape[0]
    group = seq_axis * tile_axis
    here, block_size, _ = prior_cov.shape
    width_in = proj_in.shape[1]
    depth, width_out = proj_out.shape
    rows = 2 * (block_size // width_in) * seqs
    others = max(tile_axis - 1, 1)
    halves = 2 if tok % 32 == 0 else 1
    chunks = next(c for c in (4, 2, 1) if depth % (256 * c) == 0 or c == 1)
    sub, deep = tok // halves, depth // chunks
    hbm = pl.BlockSpec(memory_space=pltpu.HBM)
    vmem = pl.BlockSpec(memory_space=pltpu.VMEM)
    return pl.pallas_call(
        functools.partial(kernel, seq_axis, tile_axis),
        out_shape=pltpu.VMEM(prior_cov.shape, F32),
        in_specs=[hbm] * 7,
        out_specs=vmem,
        scratch_shapes=[
            pltpu.SMEM(seq_lengths.shape, jnp.int32),
            pltpu.SMEM(tile_map.shape[::-1], jnp.int32),
            pltpu.VMEM(activations.shape, BF16),
            pltpu.VMEM((chunks, seqs, tok, deep), BF16),
            pltpu.VMEM(proj_in.shape, BF16),
            pltpu.VMEM((chunks, deep, width_out), BF16),
            pltpu.VMEM(prior_cov.shape, F32),
            pltpu.VMEM((width_out, tiles * rows), BF16),
            pltpu.VMEM((chunks, deep, tiles * rows), BF16),
            pltpu.VMEM((seqs * sub, tiles * rows), F32),
            pltpu.VMEM((2 * tiles * rows, seqs * sub), BF16),
            pltpu.VMEM((halves, sub, tiles * rows), F32),
            pltpu.VMEM((others, halves, sub, tiles * rows), F32),
            pltpu.VMEM((halves, seqs * sub, 2 * width_in), BF16),
            pltpu.VMEM((tiles, rows, width_in), F32),
            pltpu.VMEM((group - 1, here, rows, width_in), F32),
            pltpu.VMEM((2, 3 * seqs, block_size), F32),
            pltpu.SemaphoreType.DMA((chunks,)),
            pltpu.SemaphoreType.DMA((halves, chunks)),
            pltpu.SemaphoreType.DMA((halves,)),
            pltpu.SemaphoreType.DMA((4,)),
            pltpu.SemaphoreType.DMA((others, halves)),
            pltpu.SemaphoreType.DMA((others, halves)),
            pltpu.SemaphoreType.DMA((group - 1,)),
            pltpu.SemaphoreType.DMA((group - 1,)),
        ],
        compiler_params=pltpu.CompilerParams(
            collective_id=0, has_side_effects=True, vmem_limit_bytes=48 * 1024 * 1024
        ),
        name="grad_tiles",
    )(
        *(
            pltpu.with_memory_space_constraint(x, pltpu.HBM)
            for x in (seq_lengths, tile_map.T, activations, out_grads, proj_in, proj_out, prior_cov)
        )
    )


def solution(mesh):
    return jax.shard_map(
        functools.partial(body, mesh.shape["seq"], mesh.shape["tile"]),
        mesh=mesh,
        in_specs=(
            P("layer", "seq", "tile"),
            P("layer", "seq", "tile"),
            P(("layer", "tile"), None),
            P(("layer", "tile"), None),
            P(),
            P(),
            P(("layer", "seq", "tile"), None, None),
        ),
        out_specs=P(("layer", "seq", "tile"), None, None),
        check_vma=False,
    )
```

```python
import functools

import jax
import jax.numpy as jnp
from jax import lax
from jax.experimental import pallas as pl
from jax.experimental.pallas import tpu as pltpu
from jax.sharding import PartitionSpec as P

MESH = pl.DeviceIdType.MESH
F32 = jnp.float32
BF16 = jnp.bfloat16


def split_two(x):
    high = x.astype(BF16)
    return high, (x - high.astype(F32)).astype(BF16)


def dot(a, b):
    return jnp.dot(a, b, preferred_element_type=F32)


def kernel(
    seq_axis, tile_axis,
    lengths_hbm, map_hbm, act_hbm, grad_hbm, pin_hbm, pout_hbm, prior_hbm,
    out_ref,
    lengths, tile_map, act_v, grad_v, pin_v, pout_v, prior_v,
    select_v, total_v, picked, picked_in, acts, parts, parts_in, stacked,
    pout_sem, grad_sem, act_sem, rest_sem, pick_send, pick_recv, part_send, part_recv,
):
    seqs, tok, width = act_v.shape
    depth, width_out = pout_v.shape
    chunks = pout_sem.shape[0]
    deep = depth // chunks
    halves = act_sem.shape[0]
    sub = tok // halves
    tiles = tile_map.shape[1]
    width_in = pin_v.shape[1]
    per_block = out_ref.shape[1] // width_in
    sides = 2 * per_block
    rows = sides * seqs
    lanes = tiles * rows
    group = seq_axis * tile_axis
    here = tiles // group
    seq_me = lax.axis_index("seq")
    tile_me = lax.axis_index("tile")
    me = seq_me * tile_axis + tile_me

    def chunk(k):
        return pl.ds(pl.multiple_of(k * deep, 128), deep)

    def load_pout(k):
        return pltpu.make_async_copy(pout_hbm.at[chunk(k)], pout_v.at[chunk(k)], pout_sem.at[k])

    def load_grad(h, k):
        at = (slice(None), pl.ds(h * sub, sub), chunk(k))
        return pltpu.make_async_copy(grad_hbm.at[at], grad_v.at[at], grad_sem.at[h, k])

    def load_act(h):
        return pltpu.make_async_copy(
            act_hbm.at[:, pl.ds(h * sub, sub)], act_v.at[:, pl.ds(h * sub, sub)], act_sem.at[h]
        )

    load_map = pltpu.make_async_copy(map_hbm, tile_map, rest_sem.at[0])
    load_lengths = pltpu.make_async_copy(lengths_hbm, lengths, rest_sem.at[1])
    load_pin = pltpu.make_async_copy(pin_hbm, pin_v, rest_sem.at[2])
    load_prior = pltpu.make_async_copy(prior_hbm, prior_v, rest_sem.at[3])
    load_map.start()
    load_lengths.start()
    for h in range(halves):
        for k in range(chunks):
            if h == 0:
                load_pout(k).start()
            load_grad(h, k).start()
    load_pin.start()
    for h in range(halves):
        load_act(h).start()
    load_prior.start()

    def peer(d):
        other = lax.rem(me + d, group)
        return other, {"seq": lax.div(other, tile_axis), "tile": lax.rem(other, tile_axis)}

    barrier = pltpu.get_barrier_semaphore()
    for d in range(1, group):
        pl.semaphore_signal(barrier, inc=1, device_id=peer(d)[1], device_id_type=MESH)

    load_map.wait()
    load_lengths.wait()
    lane = lax.broadcasted_iota(jnp.int32, (1, lanes), 1)
    side = lane // seqs % sides
    wanted = jnp.zeros((1, lanes), jnp.int32)
    for k in range(tiles):
        block = jnp.where(side < per_block, tile_map[0, k], tile_map[1, k])
        wanted = jnp.where(lane // rows == k, block, wanted)
    wanted = wanted * per_block + side % per_block
    length = jnp.zeros((1, lanes), jnp.int32)
    for s in range(seqs):
        length = jnp.where(lane % seqs == s, lengths[s], length)
    scale = lax.rsqrt(length.astype(F32))
    column = lax.broadcasted_iota(jnp.int32, (width_out, lanes), 0)
    for s in range(seqs):
        match = jnp.where(column == wanted, 1.0, 0.0) * jnp.where(lane % seqs == s, 1.0, 0.0)
        select_v[s * width_out : (s + 1) * width_out, :] = match.astype(BF16)

    picks = []
    for h in range(halves):
        if h == 0:
            total_v[...] = jnp.zeros_like(total_v)

            @pl.loop(0, chunks)
            def _(k):
                load_pout(k).wait()
                load_grad(0, k).wait()
                block = grad_v[:, pl.ds(0, sub), chunk(k)].reshape(seqs * sub, deep)
                total_v[...] += dot(block, pout_v[chunk(k), :])
        else:
            for k in range(chunks):
                load_grad(h, k).wait()
            block = grad_v[:, pl.ds(h * sub, sub), :].reshape(seqs * sub, depth)
            total_v[...] = dot(block, pout_v[...])

        high, low = split_two(total_v[...])
        stack = jnp.concatenate(
            [
                jnp.concatenate([x[s * sub : (s + 1) * sub] for s in range(seqs)], axis=1)
                for x in (high, low)
            ],
            axis=0,
        )
        both = dot(stack, select_v[...])
        picked[h] = both[:sub] + both[sub:]
        if h == 0:
            pl.semaphore_wait(barrier, group - 1)
        for d in range(1, tile_axis):
            copy = pltpu.make_async_remote_copy(
                src_ref=picked.at[h],
                dst_ref=picked_in.at[d - 1, h],
                send_sem=pick_send.at[d - 1, h],
                recv_sem=pick_recv.at[d - 1, h],
                device_id={"tile": lax.rem(tile_me + d, tile_axis)},
                device_id_type=MESH,
            )
            copy.start()
            picks.append(copy)

    load_pin.wait()
    for h in range(halves):
        load_act(h).wait()
        block = act_v[:, pl.ds(h * sub, sub)].reshape(seqs * sub, width)
        split = split_two(dot(block, pin_v[...]))
        for j in range(2):
            for s in range(seqs):
                at = (j * seqs + s) * width_in
                acts[h, :, at : at + width_in] = split[j][s * sub : (s + 1) * sub]

    partial = jnp.zeros((lanes, seqs * width_in), F32)
    for h in range(halves):
        total = picked[h]
        for d in range(1, tile_axis):
            picks[h * (tile_axis - 1) + d - 1].wait_recv()
            total = total + picked_in[d - 1, h]
        position = seq_me * tok + h * sub + lax.broadcasted_iota(jnp.int32, (sub, lanes), 0)
        total = jnp.where(position < length, total * scale, 0.0)
        high, low = split_two(total.T)
        both = dot(high, acts[h])
        partial = partial + both[:, : seqs * width_in] + both[:, seqs * width_in :]
        partial = partial + dot(low, acts[h, :, : seqs * width_in])
    row = lax.broadcasted_iota(jnp.int32, (lanes, width_in), 0)
    own = jnp.zeros((lanes, width_in), F32)
    for s in range(seqs):
        own = jnp.where(row % seqs == s, partial[:, s * width_in : (s + 1) * width_in], own)
    parts[...] = own.reshape(tiles, rows, width_in)

    moves = []
    for d in range(1, group):
        other, where = peer(d)
        copy = pltpu.make_async_remote_copy(
            src_ref=parts.at[pl.ds(other * here, here)],
            dst_ref=parts_in.at[d - 1],
            send_sem=part_send.at[d - 1],
            recv_sem=part_recv.at[d - 1],
            device_id=where,
            device_id_type=MESH,
        )
        copy.start()
        moves.append(copy)

    load_prior.wait()
    total = parts[pl.ds(me * here, here)]
    for d in range(1, group):
        moves[d - 1].wait_recv()
        total = total + parts_in[d - 1]
    for k in range(here):
        pieces = [total[k, c * seqs : (c + 1) * seqs, :] for c in range(sides)]
        wide = [
            jnp.concatenate(pieces[:per_block], axis=1),
            jnp.concatenate(pieces[per_block:], axis=1),
        ]
        split = [[x.astype(F32) for x in split_two(side)] for side in wide]
        for j, part in enumerate((0, 1, 0)):
            stacked[0, j * seqs : (j + 1) * seqs, :] = split[0][part]
        for j, part in enumerate((0, 0, 1)):
            stacked[1, j * seqs : (j + 1) * seqs, :] = split[1][part]
        left = stacked[0].T.astype(BF16)
        out_ref[k] = prior_v[k] + dot(left, stacked[1].astype(BF16))
    for copy in picks:
        copy.wait_send()
    for copy in moves:
        copy.wait_send()


def body(seq_axis, tile_axis, activations, out_grads, proj_in, proj_out, seq_lengths, tile_map, prior_cov):
    seqs, tok, _ = activations.shape
    tiles = tile_map.shape[0]
    group = seq_axis * tile_axis
    here, block_size, _ = prior_cov.shape
    width_in = proj_in.shape[1]
    depth, width_out = proj_out.shape
    rows = 2 * (block_size // width_in) * seqs
    others = max(tile_axis - 1, 1)
    halves = 2 if tok % 32 == 0 else 1
    chunks = next(c for c in (4, 2, 1) if depth % (256 * c) == 0 or c == 1)
    sub = tok // halves
    hbm = pl.BlockSpec(memory_space=pltpu.HBM)
    vmem = pl.BlockSpec(memory_space=pltpu.VMEM)
    return pl.pallas_call(
        functools.partial(kernel, seq_axis, tile_axis),
        out_shape=pltpu.VMEM(prior_cov.shape, F32),
        in_specs=[hbm] * 7,
        out_specs=vmem,
        scratch_shapes=[
            pltpu.SMEM(seq_lengths.shape, jnp.int32),
            pltpu.SMEM(tile_map.shape[::-1], jnp.int32),
            pltpu.VMEM(activations.shape, BF16),
            pltpu.VMEM(out_grads.shape, BF16),
            pltpu.VMEM(proj_in.shape, BF16),
            pltpu.VMEM(proj_out.shape, BF16),
            pltpu.VMEM(prior_cov.shape, F32),
            pltpu.VMEM((seqs * width_out, tiles * rows), BF16),
            pltpu.VMEM((seqs * sub, width_out), F32),
            pltpu.VMEM((halves, sub, tiles * rows), F32),
            pltpu.VMEM((others, halves, sub, tiles * rows), F32),
            pltpu.VMEM((halves, sub, 2 * seqs * width_in), BF16),
            pltpu.VMEM((tiles, rows, width_in), F32),
            pltpu.VMEM((group - 1, here, rows, width_in), F32),
            pltpu.VMEM((2, 3 * seqs, block_size), F32),
            pltpu.SemaphoreType.DMA((chunks,)),
            pltpu.SemaphoreType.DMA((halves, chunks)),
            pltpu.SemaphoreType.DMA((halves,)),
            pltpu.SemaphoreType.DMA((4,)),
            pltpu.SemaphoreType.DMA((others, halves)),
            pltpu.SemaphoreType.DMA((others, halves)),
            pltpu.SemaphoreType.DMA((group - 1,)),
            pltpu.SemaphoreType.DMA((group - 1,)),
        ],
        compiler_params=pltpu.CompilerParams(
            collective_id=0, has_side_effects=True, vmem_limit_bytes=48 * 1024 * 1024
        ),
        name="grad_tiles",
    )(
        *(
            pltpu.with_memory_space_constraint(x, pltpu.HBM)
            for x in (seq_lengths, tile_map.T, activations, out_grads, proj_in, proj_out, prior_cov)
        )
    )


def solution(mesh):
    return jax.shard_map(
        functools.partial(body, mesh.shape["seq"], mesh.shape["tile"]),
        mesh=mesh,
        in_specs=(
            P("layer", "seq", "tile"),
            P("layer", "seq", "tile"),
            P(("layer", "tile"), None),
            P(("layer", "tile"), None),
            P(),
            P(),
            P(("layer", "seq", "tile"), None, None),
        ),
        out_specs=P(("layer", "seq", "tile"), None, None),
        check_vma=False,
    )
```

```python
import functools

import jax
import jax.numpy as jnp
from jax import lax
from jax.experimental import pallas as pl
from jax.experimental.pallas import tpu as pltpu
from jax.sharding import PartitionSpec as P

MESH = pl.DeviceIdType.MESH
F32 = jnp.float32
BF16 = jnp.bfloat16


def split_two(x):
    high = x.astype(BF16)
    return high, (x - high.astype(F32)).astype(BF16)


def dot(a, b):
    return jnp.dot(a, b, preferred_element_type=F32)


def kernel(
    seq_axis, tile_axis,
    lengths_hbm, map_hbm, act_hbm, grad_hbm, pin_hbm, pout_hbm, prior_hbm,
    out_ref,
    lengths, tile_map, act_v, grad_v, pin_v, pout_v, prior_v,
    select_v, total_v, picked, picked_in, acts, parts, parts_in, stacked,
    pout_sem, grad_sem, act_sem, rest_sem, pick_send, pick_recv, part_send, part_recv,
):
    seqs, tok, width = act_v.shape
    chunks, deep, width_out = pout_v.shape
    halves = act_sem.shape[0]
    sub = tok // halves
    tiles = tile_map.shape[1]
    width_in = pin_v.shape[1]
    per_block = out_ref.shape[1] // width_in
    sides = 2 * per_block
    rows = sides * seqs
    lanes = tiles * rows
    group = seq_axis * tile_axis
    here = tiles // group
    seq_me = lax.axis_index("seq")
    tile_me = lax.axis_index("tile")
    me = seq_me * tile_axis + tile_me

    def load_pout(k):
        return pltpu.make_async_copy(
            pout_hbm.at[pl.ds(pl.multiple_of(k * deep, 128), deep)], pout_v.at[k], pout_sem.at[k]
        )

    def load_grad(h, k):
        return pltpu.make_async_copy(
            grad_hbm.at[:, pl.ds(h * sub, sub), pl.ds(pl.multiple_of(k * deep, 128), deep)],
            grad_v.at[k, :, pl.ds(h * sub, sub)],
            grad_sem.at[h, k],
        )

    def load_act(h):
        return pltpu.make_async_copy(
            act_hbm.at[:, pl.ds(h * sub, sub)], act_v.at[:, pl.ds(h * sub, sub)], act_sem.at[h]
        )

    load_map = pltpu.make_async_copy(map_hbm, tile_map, rest_sem.at[0])
    load_lengths = pltpu.make_async_copy(lengths_hbm, lengths, rest_sem.at[1])
    load_pin = pltpu.make_async_copy(pin_hbm, pin_v, rest_sem.at[2])
    load_prior = pltpu.make_async_copy(prior_hbm, prior_v, rest_sem.at[3])
    load_map.start()
    load_lengths.start()
    for h in range(halves):
        for k in range(chunks):
            if h == 0:
                load_pout(k).start()
            load_grad(h, k).start()
    load_pin.start()
    for h in range(halves):
        load_act(h).start()
    load_prior.start()

    def peer(d):
        other = lax.rem(me + d, group)
        return other, {"seq": lax.div(other, tile_axis), "tile": lax.rem(other, tile_axis)}

    barrier = pltpu.get_barrier_semaphore()
    for d in range(1, group):
        pl.semaphore_signal(barrier, inc=1, device_id=peer(d)[1], device_id_type=MESH)

    load_map.wait()
    load_lengths.wait()
    lane = lax.broadcasted_iota(jnp.int32, (1, lanes), 1)
    side = lane // seqs % sides
    wanted = jnp.zeros((1, lanes), jnp.int32)
    for k in range(tiles):
        block = jnp.where(side < per_block, tile_map[0, k], tile_map[1, k])
        wanted = jnp.where(lane // rows == k, block, wanted)
    wanted = wanted * per_block + side % per_block
    length = jnp.zeros((1, lanes), jnp.int32)
    for s in range(seqs):
        length = jnp.where(lane % seqs == s, lengths[s], length)
    scale = lax.rsqrt(length.astype(F32))
    column = lax.broadcasted_iota(jnp.int32, (width_out, lanes), 0)
    for s in range(seqs):
        match = jnp.where(column == wanted, 1.0, 0.0) * jnp.where(lane % seqs == s, 1.0, 0.0)
        select_v[s * width_out : (s + 1) * width_out, :] = match.astype(BF16)

    picks = []
    for h in range(halves):
        total_v[...] = jnp.zeros_like(total_v)

        @pl.loop(0, chunks)
        def _(k):
            if h == 0:
                load_pout(k).wait()
            load_grad(h, k).wait()
            block = grad_v[k, :, pl.ds(h * sub, sub)].reshape(seqs * sub, deep)
            total_v[...] += dot(block, pout_v[k])

        high, low = split_two(total_v[...])
        stack = jnp.concatenate(
            [
                jnp.concatenate([x[s * sub : (s + 1) * sub] for s in range(seqs)], axis=1)
                for x in (high, low)
            ],
            axis=0,
        )
        both = dot(stack, select_v[...])
        picked[h] = both[:sub] + both[sub:]
        if h == 0:
            pl.semaphore_wait(barrier, group - 1)
        for d in range(1, tile_axis):
            copy = pltpu.make_async_remote_copy(
                src_ref=picked.at[h],
                dst_ref=picked_in.at[d - 1, h],
                send_sem=pick_send.at[d - 1, h],
                recv_sem=pick_recv.at[d - 1, h],
                device_id={"tile": lax.rem(tile_me + d, tile_axis)},
                device_id_type=MESH,
            )
            copy.start()
            picks.append(copy)

    load_pin.wait()
    @pl.loop(0, halves)
    def _(h):
        load_act(h).wait()
        block = act_v[:, pl.ds(h * sub, sub)].reshape(seqs * sub, width)
        split = split_two(dot(block, pin_v[...]))
        for j in range(2):
            for s in range(seqs):
                at = (j * seqs + s) * width_in
                acts[h, :, at : at + width_in] = split[j][s * sub : (s + 1) * sub]

    partial = jnp.zeros((lanes, seqs * width_in), F32)
    for h in range(halves):
        total = picked[h]
        for d in range(1, tile_axis):
            picks[h * (tile_axis - 1) + d - 1].wait_recv()
            total = total + picked_in[d - 1, h]
        position = seq_me * tok + h * sub + lax.broadcasted_iota(jnp.int32, (sub, lanes), 0)
        total = jnp.where(position < length, total * scale, 0.0)
        high, low = split_two(total.T)
        both = dot(high, acts[h])
        partial = partial + both[:, : seqs * width_in] + both[:, seqs * width_in :]
        partial = partial + dot(low, acts[h, :, : seqs * width_in])
    row = lax.broadcasted_iota(jnp.int32, (lanes, width_in), 0)
    own = jnp.zeros((lanes, width_in), F32)
    for s in range(seqs):
        own = jnp.where(row % seqs == s, partial[:, s * width_in : (s + 1) * width_in], own)
    parts[...] = own.reshape(tiles, rows, width_in)

    moves = []
    for d in range(1, group):
        other, where = peer(d)
        copy = pltpu.make_async_remote_copy(
            src_ref=parts.at[pl.ds(other * here, here)],
            dst_ref=parts_in.at[d - 1],
            send_sem=part_send.at[d - 1],
            recv_sem=part_recv.at[d - 1],
            device_id=where,
            device_id_type=MESH,
        )
        copy.start()
        moves.append(copy)

    load_prior.wait()
    total = parts[pl.ds(me * here, here)]
    for d in range(1, group):
        moves[d - 1].wait_recv()
        total = total + parts_in[d - 1]
    for k in range(here):
        pieces = [total[k, c * seqs : (c + 1) * seqs, :] for c in range(sides)]
        wide = [
            jnp.concatenate(pieces[:per_block], axis=1),
            jnp.concatenate(pieces[per_block:], axis=1),
        ]
        split = [[x.astype(F32) for x in split_two(side)] for side in wide]
        for j, part in enumerate((0, 1, 0)):
            stacked[0, j * seqs : (j + 1) * seqs, :] = split[0][part]
        for j, part in enumerate((0, 0, 1)):
            stacked[1, j * seqs : (j + 1) * seqs, :] = split[1][part]
        left = stacked[0].T.astype(BF16)
        out_ref[k] = prior_v[k] + dot(left, stacked[1].astype(BF16))
    for copy in picks:
        copy.wait_send()
    for copy in moves:
        copy.wait_send()


def body(seq_axis, tile_axis, activations, out_grads, proj_in, proj_out, seq_lengths, tile_map, prior_cov):
    seqs, tok, _ = activations.shape
    tiles = tile_map.shape[0]
    group = seq_axis * tile_axis
    here, block_size, _ = prior_cov.shape
    width_in = proj_in.shape[1]
    depth, width_out = proj_out.shape
    rows = 2 * (block_size // width_in) * seqs
    others = max(tile_axis - 1, 1)
    halves = 2 if tok % 32 == 0 else 1
    chunks = next(c for c in (4, 2, 1) if depth % (256 * c) == 0 or c == 1)
    sub, deep = tok // halves, depth // chunks
    hbm = pl.BlockSpec(memory_space=pltpu.HBM)
    vmem = pl.BlockSpec(memory_space=pltpu.VMEM)
    return pl.pallas_call(
        functools.partial(kernel, seq_axis, tile_axis),
        out_shape=pltpu.VMEM(prior_cov.shape, F32),
        in_specs=[hbm] * 7,
        out_specs=vmem,
        scratch_shapes=[
            pltpu.SMEM(seq_lengths.shape, jnp.int32),
            pltpu.SMEM(tile_map.shape[::-1], jnp.int32),
            pltpu.VMEM(activations.shape, BF16),
            pltpu.VMEM((chunks, seqs, tok, deep), BF16),
            pltpu.VMEM(proj_in.shape, BF16),
            pltpu.VMEM((chunks, deep, width_out), BF16),
            pltpu.VMEM(prior_cov.shape, F32),
            pltpu.VMEM((seqs * width_out, tiles * rows), BF16),
            pltpu.VMEM((seqs * sub, width_out), F32),
            pltpu.VMEM((halves, sub, tiles * rows), F32),
            pltpu.VMEM((others, halves, sub, tiles * rows), F32),
            pltpu.VMEM((halves, sub, 2 * seqs * width_in), BF16),
            pltpu.VMEM((tiles, rows, width_in), F32),
            pltpu.VMEM((group - 1, here, rows, width_in), F32),
            pltpu.VMEM((2, 3 * seqs, block_size), F32),
            pltpu.SemaphoreType.DMA((chunks,)),
            pltpu.SemaphoreType.DMA((halves, chunks)),
            pltpu.SemaphoreType.DMA((halves,)),
            pltpu.SemaphoreType.DMA((4,)),
            pltpu.SemaphoreType.DMA((others, halves)),
            pltpu.SemaphoreType.DMA((others, halves)),
            pltpu.SemaphoreType.DMA((group - 1,)),
            pltpu.SemaphoreType.DMA((group - 1,)),
        ],
        compiler_params=pltpu.CompilerParams(
            collective_id=0, has_side_effects=True, vmem_limit_bytes=48 * 1024 * 1024
        ),
        name="grad_tiles",
    )(
        *(
            pltpu.with_memory_space_constraint(x, pltpu.HBM)
            for x in (seq_lengths, tile_map.T, activations, out_grads, proj_in, proj_out, prior_cov)
        )
    )


def solution(mesh):
    return jax.shard_map(
        functools.partial(body, mesh.shape["seq"], mesh.shape["tile"]),
        mesh=mesh,
        in_specs=(
            P("layer", "seq", "tile"),
            P("layer", "seq", "tile"),
            P(("layer", "tile"), None),
            P(("layer", "tile"), None),
            P(),
            P(),
            P(("layer", "seq", "tile"), None, None),
        ),
        out_specs=P(("layer", "seq", "tile"), None, None),
        check_vma=False,
    )
```
